32 devices in a mesh: row: 2 (over x), col: 16 (over z, y, core).
Axes of the slice: x: 2, y: 2, z: 4, core: 2. Of those that a mesh axis runs over, the one named last changes fastest.
Arguments:
- density: float32 [2048, 1216], P(('row', 'col')), as said below
- pattern: int32 [32, 19], P(('row', 'col')), may hold values from 0 to 1, as said below
Outputs:
- purified: float32 [2048, 1216], P(('row', 'col'))
The draws below stay inside these ranges and needn't reach their ends.
Inputs may be any that keep to these rules, and one draw needn't show every extreme that they name: pattern[i, s] equals pattern[i + s - 9, 18 - s]; pattern[i, 9] is 1; pattern[i, s] is 0 where i + s - 9 lies outside 0 to 31. `density`: block (i, s) is zero where pattern is 0.
All inputs are finite; a program needn't handle non-finite values.
Results may differ from the reference program's by a relative error of at most 0.007.
Values may be sent and summed in bfloat16 or wider, within the bound.
No kernel may reach another device: no remote copies, remote signals or barrier semaphores. Data moves between devices by JAX's collectives and lax.ppermute only.
A program may use at most 64 MiB of HBM per device.

```python
import math
import jax
import jax.numpy as jnp

BLOCK = 64
HALF = 9
STEPS = 2
SLOTS = 19
NBLK = 32


def pattern_band(key):
    inner_key = jax.random.fold_in(key, 7)
    level_key, pick_key = jax.random.split(inner_key)
    levels = jax.random.randint(level_key, (NBLK,), 3, 9)
    pick_draw = jax.random.randint(pick_key, (NBLK, SLOTS), 0, 8)
    places = jnp.arange(NBLK)[:, None]
    offsets = jnp.arange(SLOTS)[None, :] - HALF
    partner = places + offsets
    inside = (partner >= 0) & (partner < NBLK)
    partner_safe = jnp.clip(partner, 0, NBLK - 1)
    lower_index = jnp.minimum(places, partner_safe)
    distance = jnp.abs(offsets)
    chosen = pick_draw[lower_index, HALF + distance]
    bounds = jnp.minimum(levels[places], levels[partner_safe])
    kept_flags = jnp.where(distance == 0, 1, (chosen < bounds).astype(jnp.int32))
    return jnp.where(inside, kept_flags, 0).astype(jnp.int32)


def draw_pattern(key, part):
    return pattern_band(key)


def draw_density(key, part):
    band_table = pattern_band(key)
    inner_key = jax.random.fold_in(key, 13)
    noise_key, diag_key = jax.random.split(inner_key)
    spread = 0.4 / math.sqrt(SLOTS * BLOCK)
    noise_draw = jax.random.normal(noise_key, (NBLK, SLOTS, BLOCK, BLOCK), jnp.float32)
    diagonal = jax.random.uniform(diag_key, (NBLK, BLOCK), jnp.float32, 0.2, 0.8)
    padded = jnp.pad(noise_draw, ((HALF, HALF), (0, 0), (0, 0), (0, 0)))
    mirrored = jnp.stack([jnp.swapaxes(padded[offset:offset + NBLK, 2 * HALF - offset], 1, 2) for offset in range(SLOTS)], axis=1)
    mixed = (noise_draw + mirrored) * (spread * 0.70710678)
    masked = band_table.astype(jnp.float32)[:, :, None, None] * mixed
    slot_here = jnp.arange(SLOTS)[:, None, None] == HALF
    same_entry = jnp.arange(BLOCK)[:, None] == jnp.arange(BLOCK)[None, :]
    on_diag = slot_here & same_entry[None]
    values = jnp.where(on_diag[None], diagonal[:, None, :, None], masked)
    return jnp.transpose(values, (0, 2, 1, 3)).reshape(NBLK * BLOCK, SLOTS * BLOCK).astype(jnp.float32)


def setup_inputs(seed: int = 0) -> dict:
    key_of = jax.random.split(jax.random.key(seed), 3)
    density = draw_density(jax.random.fold_in(key_of[2], 71), 0)
    pattern = draw_pattern(jax.random.fold_in(key_of[2], 71), 0)
    return {"density": density, "pattern": pattern}


def apply_mask(values, pattern_rows):
    rows_total, full_width = values.shape
    blocks = rows_total // BLOCK
    shaped = values.reshape(blocks, BLOCK, SLOTS, BLOCK)
    factor = pattern_rows.astype(values.dtype)[:, None, :, None]
    return (shaped * factor).reshape(rows_total, full_width)


def band_product(left_rows, far_rows):
    rows_total = left_rows.shape[0]
    blocks = rows_total // BLOCK
    outputs = []
    for out_slot in range(SLOTS):
        first_slot = max(0, out_slot - HALF)
        last_slot = min(2 * HALF, out_slot + HALF)
        slot_span = last_slot - first_slot + 1
        shift_start = first_slot - out_slot + HALF
        left_part = left_rows[:, first_slot * BLOCK:(last_slot + 1) * BLOCK].astype(jnp.float32).reshape(blocks, BLOCK, slot_span * BLOCK)
        right_part = far_rows[out_slot * BLOCK:out_slot * BLOCK + rows_total, shift_start * BLOCK:(shift_start + slot_span) * BLOCK].astype(jnp.float32).reshape(blocks, BLOCK, slot_span * BLOCK)
        outputs.append(jnp.einsum("iax,ibx->iab", left_part, right_part))
    return jnp.stack(outputs, axis=2).reshape(rows_total, SLOTS * BLOCK)


def reference(density, pattern):
    current = density
    for iteration in range(STEPS):
        lowered = current.astype(jnp.bfloat16)
        far_rows = jnp.pad(lowered, ((HALF * BLOCK, HALF * BLOCK), (0, 0)))
        square = apply_mask(band_product(lowered, far_rows), pattern)
        square_low = square.astype(jnp.bfloat16)
        cube_term = band_product(square_low, far_rows)
        current = apply_mask(3.0 * square - 2.0 * cube_term, pattern)
    return current
```

```python
import jax
import jax.numpy as jnp
from jax import lax
from jax.experimental import pallas as pl
from jax.experimental.pallas import tpu as pltpu
from jax.sharding import PartitionSpec as P

AXES = ("row", "col")
GROUP = 32
Z_ORDER = (0, 1, 3, 2)


def after(value, *earlier):
    return lax.optimization_barrier((value,) + earlier)[0]


def join(*parts):
    return jnp.concatenate(parts, axis=0)


def send(value, count, target):
    pairs = [(source, target(source)) for source in range(count)]
    return lax.ppermute(value, AXES, [(s, t) for s, t in pairs if 0 <= t < count])


def along_z(value, count, step):
    return send(value, count, lambda d: (d & ~12) | (((d >> 2) + step) % 4 << 2))


def first_flip(parity):
    return 2 + 14 * parity


def flip_first(value, count):
    return send(value, count, lambda d: d ^ first_flip(d & 1))


def flip_second(value, count):
    return send(value, count, lambda d: d ^ (18 - first_flip(d & 1)))


def flip_core(value, count):
    return send(value, count, lambda d: d ^ 1)


def gather(row, count):
    near = along_z(row, count, 1)
    first = flip_first(row, count)
    next_near = along_z(after(row, first), count, 3)
    pair = join(row, first)
    own = [pair, flip_second(pair, count)]
    first = flip_first(near, count)
    far = along_z(after(row, near), count, 2)
    pair = join(near, first)
    ones = [pair, flip_second(pair, count)]
    others = flip_core(after(join(*own), first), count)
    first = flip_first(after(next_near, first), count)
    pair = join(next_near, first)
    threes = [pair, flip_second(pair, count)]
    others_one = flip_core(after(join(*ones), first), count)
    first = flip_first(after(far, first, ones[1]), count)
    direct = flip_second(after(far, ones[1]), count)
    others_three = flip_core(after(join(*threes), first), count)
    last = flip_second(first, count)
    twos = [join(far, first), join(direct, last)]
    others_two = flip_core(join(*twos), count)
    return own + ones + threes + twos + [others, others_one, others_three, others_two]


def nt_dot(left, right):
    return lax.dot_general(left, right, (((1,), (1,)), ((), ())), preferred_element_type=jnp.float32)


def purify_kernel(block, half, copies, *refs):
    pieces, out_ref = refs[: 12 * copies], refs[12 * copies]
    band_ref, next_ref, flag_ref, mask_ref = refs[12 * copies + 1 :]
    slots = 2 * half + 1
    width = (slots + 1) * block
    window = (2 * half + 4) * block
    place = lax.axis_index("row") * lax.axis_size("col") + lax.axis_index("col")
    local, start = place % GROUP, place // GROUP * GROUP
    parity = local % 2
    origin = place - parity - 2 * half

    band_ref[...] = jnp.zeros_like(band_ref)
    next_ref[...] = jnp.zeros_like(next_ref)
    flag_ref[...] = jnp.zeros_like(flag_ref)
    lanes = lax.broadcasted_iota(jnp.int32, (block, 128), 1)

    def put(piece, at, index, odd):
        offset = index - origin

        @pl.when((offset >= 0) & (offset < 4 * half + 2))
        def _():
            rows = pl.ds(pl.multiple_of(offset * block, block), block)
            column = pl.multiple_of((offset + 1) // 2 * 128, 128)
            low = (1 - odd) * block
            head = piece[at : at + block, :128].astype(jnp.float32)
            tail = piece[at : at + block, width - 128 :].astype(jnp.float32)
            head_kept = lanes >= low
            tail_kept = lanes < low + block
            band_ref[rows, pl.ds(column, 128)] = jnp.where(head_kept, head, 0.0).astype(jnp.bfloat16)
            band_ref[rows, pl.ds(column + 128, width - 256)] = piece[at : at + block, 128 : width - 128]
            band_ref[rows, pl.ds(column + width - 128, 128)] = jnp.where(tail_kept, tail, 0.0).astype(jnp.bfloat16)
            number = offset - half

            @pl.when((number >= 0) & (number < 20))
            def _():
                flags = jnp.where(head_kept, 0.0, head) + jnp.where(tail_kept, 0.0, tail)
                flag_ref[pl.ds(number % 4 * 8 + number // 4, 1), :] = flags[:1]

    for copy in range(copies):
        shift = start + (0, -GROUP, GROUP)[copy]
        for core in range(2):
            odd = parity if core == 0 else 1 - parity
            flip = first_flip(odd)
            for k, step in enumerate(Z_ORDER):
                base = (local & ~13) | ((((local >> 2) & 3) + 4 - step) % 4 << 2) | odd
                for number, turned in enumerate((base, base ^ flip, base ^ (18 - flip), base ^ 18)):
                    if core == 0:
                        piece, at = pieces[12 * copy + 2 * k + number // 2], number % 2 * block
                    else:
                        piece, at = pieces[12 * copy + 8 + k], number * block
                    put(piece, at, shift + turned, odd)

    spot = lax.broadcasted_iota(jnp.int32, (128, window), 0) % block
    column_block = lax.broadcasted_iota(jnp.int32, (128, window), 1) // block
    for q in range(4):
        spread = ((column_block == spot + q) & (spot < slots)).astype(jnp.bfloat16)
        mask_ref[q] = lax.dot_general(
            flag_ref[8 * q : 8 * q + 8, :].astype(jnp.bfloat16),
            spread,
            (((1,), (0,)), ((), ())),
            preferred_element_type=jnp.float32,
        )

    def group(m, carry):
        at = pl.multiple_of(m * 4 * block, 4 * block)
        columns = pl.ds(pl.multiple_of(10 * block + at, 128), window)
        kept = jnp.concatenate(
            [jnp.broadcast_to(mask_ref[q, pl.ds(m, 1), :], (block, window)) for q in range(4)], axis=0
        )
        far = band_ref[pl.ds(at, window), columns]
        square = kept * nt_dot(band_ref[pl.ds(half * block + at, 4 * block), columns], far)
        cube = nt_dot(square.astype(jnp.bfloat16), far)
        current = kept * (3.0 * square - 2.0 * cube)
        next_ref[pl.ds(block + at, 4 * block), pl.ds(at, window)] = current.astype(jnp.bfloat16)
        return carry

    lax.fori_loop(0, 5, group, 0)
    far = next_ref[:, 8 * block : 8 * block + window]
    mine = next_ref[pl.ds(pl.multiple_of((10 + parity) * block, block), block), 8 * block : 8 * block + window]
    kept = mask_ref[pl.ds(1 + parity, 1), 2:3, :].reshape(1, window)
    square = kept * nt_dot(mine, far)
    cube = nt_dot(square.astype(jnp.bfloat16), far)
    current = kept * (3.0 * square - 2.0 * cube)
    out_ref[...] = jnp.where(
        parity == 0,
        current[:, block : block + slots * block],
        current[:, 2 * block : 2 * block + slots * block],
    )


def local(density, pattern):
    block, width = density.shape
    slots = pattern.shape[1]
    half = (slots - 1) // 2
    count = lax.axis_size("row") * lax.axis_size("col")
    place = lax.axis_index("row") * lax.axis_size("col") + lax.axis_index("col")
    flags = jnp.broadcast_to(pattern.astype(jnp.bfloat16), (block, slots))
    flags = jnp.pad(flags, ((0, 0), (0, block - slots)))
    low = density.astype(jnp.bfloat16)
    row = jnp.where(
        place % 2 == 0,
        jnp.concatenate([flags, low], axis=1),
        jnp.concatenate([low, flags], axis=1),
    )
    pieces = gather(row, count)
    copies = 1
    if count > GROUP:
        pieces = (
            pieces
            + [send(piece, count, lambda d: d + GROUP) for piece in pieces]
            + [send(piece, count, lambda d: d - GROUP) for piece in pieces]
        )
        copies = 3

    def kernel(*refs):
        purify_kernel(block, half, copies, *refs)

    window = (2 * half + 4) * block
    return pl.pallas_call(
        kernel,
        out_shape=jax.ShapeDtypeStruct((block, width), jnp.float32),
        in_specs=[pl.BlockSpec(memory_space=pltpu.VMEM)] * len(pieces),
        out_specs=pl.BlockSpec(memory_space=pltpu.VMEM),
        scratch_shapes=[
            pltpu.VMEM(((4 * half + 2) * block, (6 * half + 4) * block), jnp.bfloat16),
            pltpu.VMEM((window, (4 * half + 2) * block), jnp.bfloat16),
            pltpu.VMEM((32, 128), jnp.float32),
            pltpu.VMEM((4, 8, window), jnp.float32),
        ],
        compiler_params=pltpu.CompilerParams(vmem_limit_bytes=56 * 2**20),
    )(*pieces)


def solution(mesh):
    placed = (P(AXES, None), P(AXES, None))
    return jax.shard_map(local, mesh=mesh, in_specs=placed, out_specs=P(AXES, None), check_vma=False)
```

```python
import jax
import jax.numpy as jnp
from jax import lax
from jax.experimental import pallas as pl
from jax.experimental.pallas import tpu as pltpu
from jax.sharding import PartitionSpec as P

AXES = ("row", "col")
GROUP = 32
Z_ORDER = (0, 1, 3, 2)


def after(value, *earlier):
    return lax.optimization_barrier((value,) + earlier)[0]


def join(*parts):
    return jnp.concatenate(parts, axis=0)


def send(value, count, target):
    pairs = [(source, target(source)) for source in range(count)]
    return lax.ppermute(value, AXES, [(s, t) for s, t in pairs if 0 <= t < count])


def along_z(value, count, step):
    return send(value, count, lambda d: (d & ~12) | (((d >> 2) + step) % 4 << 2))


def first_flip(parity):
    return 2 + 14 * parity


def flip_first(value, count):
    return send(value, count, lambda d: d ^ first_flip(d & 1))


def flip_second(value, count):
    return send(value, count, lambda d: d ^ (18 - first_flip(d & 1)))


def flip_core(value, count):
    return send(value, count, lambda d: d ^ 1)


def gather(row, count):
    near = along_z(row, count, 1)
    first = flip_first(row, count)
    next_near = along_z(after(row, first), count, 3)
    far = along_z(after(row, near), count, 2)
    pieces = [row, first, flip_second(join(row, first), count)]
    first = flip_first(near, count)
    pieces += [near, first, flip_second(join(near, first), count)]
    first = flip_first(next_near, count)
    pieces += [next_near, first, flip_second(join(next_near, first), count)]
    first = flip_first(far, count)
    pieces += [far, first, flip_second(far, count), flip_second(first, count)]
    return pieces + [flip_core(piece, count) for piece in pieces]


def dot(left, right, on=0):
    return lax.dot_general(left, right, (((1,), (on,)), ((), ())), preferred_element_type=jnp.float32)


def purify_kernel(block, half, copies, *refs):
    count = len(refs) - 7
    pieces, out_ref = refs[:count], refs[count]
    band_ref, next_ref, flag_ref, mask_ref, square_ref, low_ref = refs[count + 1 :]
    slots = 2 * half + 1
    width = (slots + 1) * block
    reach = 4 * half + 2
    window = (2 * half + 4) * block
    panel = 4 * block
    bits = jnp.bfloat16
    place = lax.axis_index("row") * lax.axis_size("col") + lax.axis_index("col")
    local, start = place % GROUP, place // GROUP * GROUP
    parity = local % 2
    origin = place - parity - 2 * half

    left = 10 * block
    band_ref[:, left : left + reach * block] = jnp.zeros((reach * block, reach * block), bits)
    flag_ref[...] = jnp.zeros_like(flag_ref)
    next_ref[...] = jnp.zeros_like(next_ref)
    lanes = lax.broadcasted_iota(jnp.int32, (block, 128), 1)

    def put(piece, index, odd):
        offset = index - origin

        @pl.when((offset >= 0) & (offset < reach))
        def _():
            rows = pl.ds(pl.multiple_of(offset * block, block), block)
            column = pl.multiple_of((offset + 1) // 2 * 128, 128)
            low = (1 - odd) * block
            head = piece[:, :128].astype(jnp.float32)
            tail = piece[:, width - 128 :].astype(jnp.float32)
            head_kept = lanes >= low
            tail_kept = lanes < low + block
            band_ref[rows, pl.ds(column, 128)] = jnp.where(head_kept, head, 0.0).astype(bits)
            band_ref[rows, pl.ds(column + 128, width - 256)] = piece[:, 128 : width - 128]
            band_ref[rows, pl.ds(column + width - 128, 128)] = jnp.where(tail_kept, tail, 0.0).astype(bits)
            flags = jnp.where(head_kept, 0.0, head) + jnp.where(tail_kept, 0.0, tail)
            flag_ref[pl.ds(offset, 1), :] = flags[:1]

    each = count // copies
    for copy in range(copies):
        shift = start + (0, -GROUP, GROUP)[copy]
        held = [
            piece.at[pl.ds(at, block), :]
            for piece in pieces[each * copy : each * copy + each]
            for at in range(0, piece.shape[0], block)
        ]
        for core in range(2):
            odd = parity if core == 0 else 1 - parity
            flip = first_flip(odd)
            for k, step in enumerate(Z_ORDER):
                base = (local & ~13) | ((((local >> 2) & 3) + 4 - step) % 4 << 2) | odd
                for number, turned in enumerate((base, base ^ flip, base ^ (18 - flip), base ^ 18)):
                    put(held[16 * core + 4 * k + number], shift + turned, odd)

    shape = (128, mask_ref.shape[1])
    lane = lax.broadcasted_iota(jnp.int32, shape, 0)
    slot = lane % block
    spread = (lax.broadcasted_iota(jnp.int32, shape, 1) // block == slot + lane // block + 4) & (slot < slots)
    mask_ref[...] = dot(flag_ref[...].astype(bits), spread.astype(bits))

    chunks = ((0, 2 * panel, 0, 5 * panel), (2 * panel, 2 * panel, 0, window), (4 * panel, window - 4 * panel, panel, window))

    def group(m, carry):
        at = pl.multiple_of(m * panel, panel)

        def kept(n, size):
            rows = []
            for w in range(n // block, (n + size) // block):
                column = (22 + w % 2 - w) * block
                row = mask_ref[pl.ds(4 * m + w, 1), column : column + panel]
                rows.append(jnp.broadcast_to(row, (block, panel)))
            return jnp.concatenate(rows, axis=0)

        def rows(first, size, low, high):
            return band_ref[pl.ds(at + first, size), pl.ds(pl.multiple_of(left + at + low, 128), high - low)]

        for n, size, low, high in chunks:
            square = kept(n, size) * dot(rows(n, size, low, high), rows(half * block, panel, low, high), 1)
            square_ref[n : n + size, :] = square
            low_ref[n : n + size, :] = square.astype(bits)
        for n, size, low, high in chunks:
            cube = dot(rows(n, size, low, high), low_ref[low:high, :])
            current = kept(n, size) * (3.0 * square_ref[n : n + size, :] - 2.0 * cube)
            next_ref[pl.ds(at + n, size), pl.ds(pl.multiple_of(at + 2 * block, 128), panel)] = current.astype(bits)
        return carry

    lax.fori_loop(0, 5, group, 0)

    inner = slice(half * block, (half + 20) * block)
    chosen = lax.broadcasted_iota(jnp.int32, (block, panel), 1)
    chosen = chosen == lax.broadcasted_iota(jnp.int32, (block, panel), 0) + (1 + parity) * block
    mine = dot(chosen.astype(bits), next_ref[inner, 10 * block : 14 * block], 1).astype(bits)
    kept = mask_ref[pl.ds(2 * half + parity, 1), 2 * block : 2 * block + window]
    square = kept * dot(mine, next_ref[inner, :])
    cube = dot(square.astype(bits)[:, 2 * block :], next_ref[inner, :])
    current = kept * (3.0 * square - 2.0 * cube)
    out_ref[...] = jnp.where(
        parity == 0,
        current[:, 2 * block : (slots + 2) * block],
        current[:, 3 * block : (slots + 3) * block],
    )


def local(density, pattern):
    block, width = density.shape
    slots = pattern.shape[1]
    half = (slots - 1) // 2
    count = lax.axis_size("row") * lax.axis_size("col")
    place = lax.axis_index("row") * lax.axis_size("col") + lax.axis_index("col")
    flags = jnp.broadcast_to(pattern.astype(jnp.bfloat16), (block, slots))
    flags = jnp.pad(flags, ((0, 0), (0, block - slots)))
    low = density.astype(jnp.bfloat16)
    row = jnp.where(
        place % 2 == 0,
        jnp.concatenate([flags, low], axis=1),
        jnp.concatenate([low, flags], axis=1),
    )
    pieces = gather(row, count)
    copies = 1
    if count > GROUP:
        pieces = (
            pieces
            + [send(piece, count, lambda d: d + GROUP) for piece in pieces]
            + [send(piece, count, lambda d: d - GROUP) for piece in pieces]
        )
        copies = 3

    def kernel(*refs):
        purify_kernel(block, half, copies, *refs)

    window = (2 * half + 4) * block
    reach = (4 * half + 2) * block
    return pl.pallas_call(
        kernel,
        out_shape=jax.ShapeDtypeStruct((block, width), jnp.float32),
        in_specs=[pl.BlockSpec(memory_space=pltpu.VMEM)] * len(pieces),
        out_specs=pl.BlockSpec(memory_space=pltpu.VMEM),
        scratch_shapes=[
            pltpu.VMEM((reach, (6 * half + 4) * block), jnp.bfloat16),
            pltpu.VMEM((reach, window), jnp.bfloat16),
            pltpu.VMEM((40, 128), jnp.float32),
            pltpu.VMEM((40, 26 * block), jnp.float32),
            pltpu.VMEM((window, 4 * block), jnp.float32),
            pltpu.VMEM((window, 4 * block), jnp.bfloat16),
        ],
        compiler_params=pltpu.CompilerParams(vmem_limit_bytes=36 * 2**20),
    )(*pieces)


def solution(mesh):
    placed = (P(AXES, None), P(AXES, None))
    return jax.shard_map(local, mesh=mesh, in_specs=placed, out_specs=P(AXES, None), check_vma=False)
```

```python
import jax
import jax.numpy as jnp
from jax import lax
from jax.experimental import pallas as pl
from jax.experimental.pallas import tpu as pltpu
from jax.sharding import PartitionSpec as P

AXES = ("row", "col")
GROUP = 32
HELD = ((0, 1, 0), (0, 0, 1), (0, 1, 1), (2, 0, 0), (1, 0, 0), (3, 0, 0), (1, 1, 0), (3, 1, 0))
HELD += ((1, 0, 1), (3, 0, 1), (1, 1, 1), (3, 1, 1), (2, 1, 0), (2, 0, 1), (2, 1, 1), (0, 0, 0))


def after(value, *earlier):
    return lax.optimization_barrier((value,) + earlier)[0]


def join(*parts):
    return jnp.concatenate(parts, axis=0)


def send(value, count, target):
    pairs = [(source, target(source)) for source in range(count)]
    return lax.ppermute(value, AXES, [(s, t) for s, t in pairs if 0 <= t < count])


def along_z(value, count, step):
    return send(value, count, lambda d: (d & ~12) | (((d >> 2) + step) % 4 << 2))


def first_flip(parity):
    return 2 + 14 * parity


def flip_first(value, count):
    return send(value, count, lambda d: d ^ first_flip(d & 1))


def flip_second(value, count):
    return send(value, count, lambda d: d ^ (18 - first_flip(d & 1)))


def flip_core(value, count):
    return send(value, count, lambda d: d ^ 1)


def gather(row, count):
    first = flip_first(row, count)
    near = along_z(row, count, 1)
    next_near = along_z(row, count, 3)
    second = flip_second(join(row, first), count)
    far = along_z(after(row, first), count, 2)
    pair = join(near, next_near)
    pair_first = flip_first(after(pair, second), count)
    pair_second = flip_second(after(pair, second), count)
    pair_last = flip_second(pair_first, count)
    far_first = flip_first(far, count)
    far_second = flip_second(far, count)
    far_last = flip_second(far_first, count)
    pieces = [first, second, far, pair, pair_first, pair_second, pair_last, far_first, far_second, far_last, row]
    return pieces + [flip_core(piece, count) for piece in pieces]


def dot(left, right, on=0):
    return lax.dot_general(left, right, (((1,), (on,)), ((), ())), preferred_element_type=jnp.float32)


def purify_kernel(block, half, copies, *refs):
    count = len(refs) - 7
    pieces, out_ref = refs[:count], refs[count]
    band_ref, next_ref, flag_ref, mask_ref, square_ref, low_ref = refs[count + 1 :]
    slots = 2 * half + 1
    width = (slots + 1) * block
    reach = 4 * half + 2
    window = (2 * half + 4) * block
    panel = 4 * block
    bits = jnp.bfloat16
    place = lax.axis_index("row") * lax.axis_size("col") + lax.axis_index("col")
    local, start = place % GROUP, place // GROUP * GROUP
    parity = local % 2
    origin = place - parity - 2 * half

    left = 10 * block
    band_ref[:, left : left + reach * block] = jnp.zeros((reach * block, reach * block), bits)
    flag_ref[...] = jnp.zeros_like(flag_ref)
    next_ref[...] = jnp.zeros_like(next_ref)
    lanes = lax.broadcasted_iota(jnp.int32, (block, 128), 1)

    def put(piece, index, odd):
        offset = index - origin

        @pl.when((offset >= 0) & (offset < reach))
        def _():
            rows = pl.ds(pl.multiple_of(offset * block, block), block)
            column = pl.multiple_of((offset + 1) // 2 * 128, 128)
            low = (1 - odd) * block
            head = piece[:, :128].astype(jnp.float32)
            tail = piece[:, width - 128 :].astype(jnp.float32)
            head_kept = lanes >= low
            tail_kept = lanes < low + block
            band_ref[rows, pl.ds(column, 128)] = jnp.where(head_kept, head, 0.0).astype(bits)
            band_ref[rows, pl.ds(column + 128, width - 256)] = piece[:, 128 : width - 128]
            band_ref[rows, pl.ds(column + width - 128, 128)] = jnp.where(tail_kept, tail, 0.0).astype(bits)
            flags = jnp.where(head_kept, 0.0, head) + jnp.where(tail_kept, 0.0, tail)
            flag_ref[pl.ds(offset, 1), :] = flags[:1]

    each = count // copies
    for copy in range(copies):
        shift = start + (0, -GROUP, GROUP)[copy]
        held = [
            piece.at[pl.ds(at, block), :]
            for piece in pieces[each * copy : each * copy + each]
            for at in range(0, piece.shape[0], block)
        ]
        for core in range(2):
            odd = parity if core == 0 else 1 - parity
            flip = first_flip(odd)
            for number, (step, one, two) in enumerate(HELD):
                base = (local & ~13) | ((((local >> 2) & 3) + 4 - step) % 4 << 2) | odd
                put(held[16 * core + number], shift + (base ^ (one * flip + two * (18 - flip))), odd)

    shape = (128, mask_ref.shape[1])
    lane = lax.broadcasted_iota(jnp.int32, shape, 0)
    slot = lane % block
    spread = (lax.broadcasted_iota(jnp.int32, shape, 1) // block == slot + lane // block + 4) & (slot < slots)
    mask_ref[...] = dot(flag_ref[...].astype(bits), spread.astype(bits))

    def spans():
        for n in range(0, window, panel):
            size = min(panel, window - n)
            low = max(0, n - half * block) // 128 * 128
            high = min(window, -(-(n + size + half * block) // 128) * 128)
            yield n, size, low, high

    for m in range(5):
        at = m * panel

        def kept(n, size):
            rows = []
            for w in range(n // block, (n + size) // block):
                column = (22 + w % 2 - w) * block
                row = mask_ref[4 * m + w : 4 * m + w + 1, column : column + panel]
                rows.append(jnp.broadcast_to(row, (block, panel)))
            return jnp.concatenate(rows, axis=0)

        def rows(first, size, low, high):
            return band_ref[at + first : at + first + size, left + at + low : left + at + high]

        for n, size, low, high in spans():
            square = kept(n, size) * dot(rows(n, size, low, high), rows(half * block, panel, low, high), 1)
            square_ref[n : n + size, :] = square
            low_ref[n : n + size, :] = square.astype(bits)
        for n, size, low, high in spans():
            if half * block < at + n + size and at + n < (half + 20) * block:
                cube = dot(rows(n, size, low, high), low_ref[low:high, :])
                current = kept(n, size) * (3.0 * square_ref[n : n + size, :] - 2.0 * cube)
                next_ref[at + n : at + n + size, at + 2 * block : at + 2 * block + panel] = current.astype(bits)

    inner = slice(half * block, (half + 20) * block)
    chosen = lax.broadcasted_iota(jnp.int32, (block, panel), 1)
    chosen = chosen == lax.broadcasted_iota(jnp.int32, (block, panel), 0) + (1 + parity) * block
    mine = dot(chosen.astype(bits), next_ref[inner, 10 * block : 14 * block], 1).astype(bits)
    kept = mask_ref[pl.ds(2 * half + parity, 1), 2 * block : 2 * block + window]
    square = kept * dot(mine, next_ref[inner, :])
    cube = dot(square.astype(bits)[:, 2 * block :], next_ref[inner, :])
    current = kept * (3.0 * square - 2.0 * cube)
    out_ref[...] = jnp.where(
        parity == 0,
        current[:, 2 * block : (slots + 2) * block],
        current[:, 3 * block : (slots + 3) * block],
    )


def local(density, pattern):
    block, width = density.shape
    slots = pattern.shape[1]
    half = (slots - 1) // 2
    count = lax.axis_size("row") * lax.axis_size("col")
    place = lax.axis_index("row") * lax.axis_size("col") + lax.axis_index("col")
    flags = jnp.broadcast_to(pattern.astype(jnp.bfloat16), (block, slots))
    flags = jnp.pad(flags, ((0, 0), (0, block - slots)))
    low = density.astype(jnp.bfloat16)
    row = jnp.where(
        place % 2 == 0,
        jnp.concatenate([flags, low], axis=1),
        jnp.concatenate([low, flags], axis=1),
    )
    pieces = gather(row, count)
    copies = 1
    if count > GROUP:
        pieces = (
            pieces
            + [send(piece, count, lambda d: d + GROUP) for piece in pieces]
            + [send(piece, count, lambda d: d - GROUP) for piece in pieces]
        )
        copies = 3

    def kernel(*refs):
        purify_kernel(block, half, copies, *refs)

    window = (2 * half + 4) * block
    reach = (4 * half + 2) * block
    return pl.pallas_call(
        kernel,
        out_shape=jax.ShapeDtypeStruct((block, width), jnp.float32),
        in_specs=[pl.BlockSpec(memory_space=pltpu.VMEM)] * len(pieces),
        out_specs=pl.BlockSpec(memory_space=pltpu.VMEM),
        scratch_shapes=[
            pltpu.VMEM((reach, (6 * half + 4) * block), jnp.bfloat16),
            pltpu.VMEM((reach, window), jnp.bfloat16),
            pltpu.VMEM((40, 128), jnp.float32),
            pltpu.VMEM((40, 26 * block), jnp.float32),
            pltpu.VMEM((window, 4 * block), jnp.float32),
            pltpu.VMEM((window, 4 * block), jnp.bfloat16),
        ],
        compiler_params=pltpu.CompilerParams(vmem_limit_bytes=36 * 2**20),
    )(*pieces)


def solution(mesh):
    placed = (P(AXES, None), P(AXES, None))
    return jax.shard_map(local, mesh=mesh, in_specs=placed, out_specs=P(AXES, None), check_vma=False)
```

```python
import jax
import jax.numpy as jnp
from jax import lax
from jax.experimental import pallas as pl
from jax.experimental.pallas import tpu as pltpu
from jax.sharding import PartitionSpec as P

AXES = ("row", "col")
GROUP = 32
HELD = ((0, 1, 0), (0, 0, 1), (0, 1, 1), (2, 0, 0), (1, 0, 0), (3, 0, 0), (1, 1, 0), (3, 1, 0))
HELD += ((1, 0, 1), (3, 0, 1), (1, 1, 1), (3, 1, 1), (2, 1, 0), (2, 0, 1), (2, 1, 1), (0, 0, 0))


def after(value, *earlier):
    return lax.optimization_barrier((value,) + earlier)[0]


def join(*parts):
    return jnp.concatenate(parts, axis=0)


def send(value, count, target):
    pairs = [(source, target(source)) for source in range(count)]
    return lax.ppermute(value, AXES, [(s, t) for s, t in pairs if 0 <= t < count])


def along_z(value, count, step):
    return send(value, count, lambda d: (d & ~12) | (((d >> 2) + step) % 4 << 2))


def first_flip(parity):
    return 2 + 14 * parity


def flip_first(value, count):
    return send(value, count, lambda d: d ^ first_flip(d & 1))


def flip_second(value, count):
    return send(value, count, lambda d: d ^ (18 - first_flip(d & 1)))


def flip_core(value, count):
    return send(value, count, lambda d: d ^ 1)


def gather(row, count):
    first = flip_first(row, count)
    near = along_z(row, count, 1)
    next_near = along_z(row, count, 3)
    second = flip_second(join(row, first), count)
    far = along_z(after(row, first), count, 2)
    pair = join(near, next_near)
    pair_first = flip_first(after(pair, second), count)
    pair_second = flip_second(after(pair, second), count)
    pair_last = flip_second(pair_first, count)
    far_first = flip_first(far, count)
    far_second = flip_second(far, count)
    far_last = flip_second(far_first, count)
    pieces = [first, second, far, pair, pair_first, pair_second, pair_last, far_first, far_second, far_last, row]
    return pieces + [flip_core(piece, count) for piece in pieces]


def prepare_kernel(density_ref, pattern_ref, row_ref):
    block, width = density_ref.shape
    slots = pattern_ref.shape[1]
    flags = jnp.concatenate(
        [pattern_ref[...].astype(jnp.float32), jnp.zeros((1, block - slots), jnp.float32)], axis=1
    )
    flags = jnp.broadcast_to(flags, (block, block)).astype(jnp.bfloat16)
    parity = (lax.axis_index("row") * lax.axis_size("col") + lax.axis_index("col")) % 2
    low = density_ref[...].astype(jnp.bfloat16)

    @pl.when(parity == 0)
    def _():
        row_ref[:, :block] = flags
        row_ref[:, block:] = low

    @pl.when(parity == 1)
    def _():
        row_ref[:, :width] = low
        row_ref[:, width:] = flags


def dot(left, right, on=0):
    return lax.dot_general(left, right, (((1,), (on,)), ((), ())), preferred_element_type=jnp.float32)


def purify_kernel(block, half, copies, *refs):
    count = len(refs) - 7
    pieces, out_ref = refs[:count], refs[count]
    band_ref, next_ref, flag_ref, mask_ref, square_ref, low_ref = refs[count + 1 :]
    slots = 2 * half + 1
    width = (slots + 1) * block
    reach = 4 * half + 2
    window = (2 * half + 4) * block
    panel = 4 * block
    bits = jnp.bfloat16
    place = lax.axis_index("row") * lax.axis_size("col") + lax.axis_index("col")
    local, start = place % GROUP, place // GROUP * GROUP
    parity = local % 2
    origin = place - parity - 2 * half

    left = 10 * block
    flag_ref[...] = jnp.zeros_like(flag_ref)

    def clear(ref, row, first, last, column):
        if first < last:
            shape = (block, (last - first) * block)
            ref[row * block : (row + 1) * block, column + first * block : column + last * block] = jnp.zeros(shape, bits)

    for row in range(reach):
        first, tile = (row + 1) // 2 * 2 - half - 1, (row - half) // 4 * 4
        clear(band_ref, row, max(0, tile), max(0, first), left)
        clear(band_ref, row, min(reach, first + slots + 1), min(reach, tile + 2 * half + 4), left)

        @pl.when((origin + row < 0) | (origin + row >= lax.axis_size("row") * lax.axis_size("col")))
        def _():
            clear(band_ref, row, first, first + slots + 1, left)

    for row in range(half, half + 20):
        clear(next_ref, row, 0, 2, 0)
        for m in range(5):
            if not 4 * m <= row < 4 * m + 2 * half + 4:
                clear(next_ref, row, 4 * m + 2, 4 * m + 6, 0)
    lanes = lax.broadcasted_iota(jnp.int32, (block, 128), 1)

    def put(piece, index, odd):
        offset = index - origin

        @pl.when((offset >= 0) & (offset < reach))
        def _():
            rows = pl.ds(pl.multiple_of(offset * block, block), block)
            column = pl.multiple_of((offset + 1) // 2 * 128, 128)
            low = (1 - odd) * block
            head = piece[:, :128].astype(jnp.float32)
            tail = piece[:, width - 128 :].astype(jnp.float32)
            head_kept = lanes >= low
            tail_kept = lanes < low + block
            band_ref[rows, pl.ds(column, 128)] = jnp.where(head_kept, head, 0.0).astype(bits)
            band_ref[rows, pl.ds(column + 128, width - 256)] = piece[:, 128 : width - 128]
            band_ref[rows, pl.ds(column + width - 128, 128)] = jnp.where(tail_kept, tail, 0.0).astype(bits)
            flags = jnp.where(head_kept, 0.0, head) + jnp.where(tail_kept, 0.0, tail)
            flag_ref[pl.ds(offset, 1), :] = flags[:1]

    each = count // copies
    for copy in range(copies):
        shift = start + (0, -GROUP, GROUP)[copy]
        held = [
            piece.at[pl.ds(at, block), :]
            for piece in pieces[each * copy : each * copy + each]
            for at in range(0, piece.shape[0], block)
        ]
        for core in range(2):
            odd = parity if core == 0 else 1 - parity
            flip = first_flip(odd)
            for number, (step, one, two) in enumerate(HELD):
                base = (local & ~13) | ((((local >> 2) & 3) + 4 - step) % 4 << 2) | odd
                put(held[16 * core + number], shift + (base ^ (one * flip + two * (18 - flip))), odd)

    shape = (128, mask_ref.shape[1])
    lane = lax.broadcasted_iota(jnp.int32, shape, 0)
    slot = lane % block
    spread = (lax.broadcasted_iota(jnp.int32, shape, 1) // block == slot + lane // block + 4) & (slot < slots)
    mask_ref[...] = dot(flag_ref[...].astype(bits), spread.astype(bits))

    spans = [(0, 1, 0, 10), (1, 4, 0, 14), (5, 4, 0, 18), (9, 4, 0, 22), (13, 4, 4, 22), (17, 4, 8, 22), (21, 1, 12, 22)]

    for m in range(5):

        def kept(first, size):
            rows = []
            for w in range(first, first + size):
                column = (22 + w % 2 - w) * block
                row = mask_ref[4 * m + w : 4 * m + w + 1, column : column + panel]
                rows.append(jnp.broadcast_to(row, (block, panel)))
            return jnp.concatenate(rows, axis=0)

        def rows(first, size, low, high):
            at = 4 * m * block
            columns = slice(left + at + low * block, left + at + high * block)
            return band_ref[at + first * block : at + (first + size) * block, columns]

        for step, (first, size, low, high) in enumerate(spans):
            span = slice(first * block, (first + size) * block)
            other = m + step - 3
            if size == 4 and 0 <= other < m:
                mirrored = (9 + 4 * (m - other)) * block
                square = square_ref[other, mirrored : mirrored + panel, :].T
            else:
                square = kept(first, size) * dot(rows(first, size, low, high), rows(half, 4, low, high), 1)
            square_ref[m, span, :] = square
            low_ref[m, span, :] = square.astype(bits)
        for first, size, low, high in spans:
            if half <= 4 * m + first < half + 20:
                span = slice(first * block, (first + size) * block)
                cube = dot(rows(first, size, low, high), low_ref[m, low * block : high * block, :])
                current = kept(first, size) * (3.0 * square_ref[m, span, :] - 2.0 * cube)
                at = 4 * m * block
                next_ref[at + span.start : at + span.stop, at + 2 * block : at + 6 * block] = current.astype(bits)

    inner = slice(half * block, (half + 20) * block)
    chosen = lax.broadcasted_iota(jnp.int32, (block, panel), 1)
    chosen = chosen == lax.broadcasted_iota(jnp.int32, (block, panel), 0) + (1 + parity) * block
    mine = dot(chosen.astype(bits), next_ref[inner, 10 * block : 14 * block], 1).astype(bits)
    kept = mask_ref[pl.ds(2 * half + parity, 1), 2 * block : 2 * block + window]

    def times_next(value):
        parts = []
        for n in range(0, window, panel):
            low = max(0, n // block - half - 2) // 2 * 2 * block
            high = min(20, -(-(n // block + half + 2) // 2) * 2) * block
            rows = slice(half * block + low, half * block + high)
            parts.append(dot(value[:, low:high], next_ref[rows, n : min(n + panel, window)]))
        return jnp.concatenate(parts, axis=1)

    square = kept * times_next(mine)
    cube = times_next(square.astype(bits)[:, 2 * block :])
    current = kept * (3.0 * square - 2.0 * cube)
    out_ref[...] = jnp.where(
        parity == 0,
        current[:, 2 * block : (slots + 2) * block],
        current[:, 3 * block : (slots + 3) * block],
    )


def local(density, pattern):
    block, width = density.shape
    slots = pattern.shape[1]
    half = (slots - 1) // 2
    count = lax.axis_size("row") * lax.axis_size("col")
    row = pl.pallas_call(
        prepare_kernel,
        out_shape=pltpu.VMEM((block, width + block), jnp.bfloat16),
        in_specs=[pl.BlockSpec(memory_space=pltpu.VMEM)] * 2,
        out_specs=pl.BlockSpec(memory_space=pltpu.VMEM),
    )(density, pattern)
    pieces = gather(row, count)
    copies = 1
    if count > GROUP:
        pieces = (
            pieces
            + [send(piece, count, lambda d: d + GROUP) for piece in pieces]
            + [send(piece, count, lambda d: d - GROUP) for piece in pieces]
        )
        copies = 3

    def kernel(*refs):
        purify_kernel(block, half, copies, *refs)

    window = (2 * half + 4) * block
    reach = (4 * half + 2) * block
    return pl.pallas_call(
        kernel,
        out_shape=jax.ShapeDtypeStruct((block, width), jnp.float32),
        in_specs=[pl.BlockSpec(memory_space=pltpu.VMEM)] * len(pieces),
        out_specs=pl.BlockSpec(memory_space=pltpu.VMEM),
        scratch_shapes=[
            pltpu.VMEM((reach, (6 * half + 4) * block), jnp.bfloat16),
            pltpu.VMEM((reach, window), jnp.bfloat16),
            pltpu.VMEM((40, 128), jnp.float32),
            pltpu.VMEM((40, 26 * block), jnp.float32),
            pltpu.VMEM((5, window, 4 * block), jnp.float32),
            pltpu.VMEM((5, window, 4 * block), jnp.bfloat16),
        ],
        compiler_params=pltpu.CompilerParams(vmem_limit_bytes=44 * 2**20),
    )(*pieces)


def solution(mesh):
    placed = (P(AXES, None), P(AXES, None))
    return jax.shard_map(local, mesh=mesh, in_specs=placed, out_specs=P(AXES, None), check_vma=False)
```

```python
import jax
import jax.numpy as jnp
from jax import lax
from jax.experimental import pallas as pl
from jax.experimental.pallas import tpu as pltpu
from jax.sharding import PartitionSpec as P

AXES = ("row", "col")
GROUP = 32
HELD = ((0, 1, 0), (0, 0, 1), (0, 1, 1), (2, 0, 0), (1, 0, 0), (3, 0, 0), (1, 1, 0), (3, 1, 0))
HELD += ((1, 0, 1), (3, 0, 1), (1, 1, 1), (3, 1, 1), (2, 1, 0), (2, 0, 1), (2, 1, 1), (0, 0, 0))


def after(value, *earlier):
    return lax.optimization_barrier((value,) + earlier)[0]


def join(*parts):
    return jnp.concatenate(parts, axis=0)


def send(value, count, target):
    pairs = [(source, target(source)) for source in range(count)]
    return lax.ppermute(value, AXES, [(s, t) for s, t in pairs if 0 <= t < count])


def along_z(value, count, step):
    return send(value, count, lambda d: (d & ~12) | (((d >> 2) + step) % 4 << 2))


def first_flip(parity):
    return 2 + 14 * parity


def flip_first(value, count):
    return send(value, count, lambda d: d ^ first_flip(d & 1))


def flip_second(value, count):
    return send(value, count, lambda d: d ^ (18 - first_flip(d & 1)))


def flip_core(value, count):
    return send(value, count, lambda d: d ^ 1)


def gather(row, count):
    first = flip_first(row, count)
    near = along_z(row, count, 1)
    next_near = along_z(row, count, 3)
    second = flip_second(join(row, first), count)
    far = along_z(after(row, first), count, 2)
    far_last = along_z(second[second.shape[0] // 2 :], count, 2)
    pair = join(near, next_near)
    pair_first = flip_first(pair, count)
    pair_second = flip_second(after(pair, second), count)
    pair_last = flip_second(pair_first, count)
    far_first = flip_first(far, count)
    far_second = flip_second(far, count)
    pieces = [first, second, far, pair, pair_first, pair_second, pair_last, far_first, far_second, far_last, row]
    return pieces + [flip_core(after(piece, far_last) if piece is pair_first else piece, count) for piece in pieces]


def prepare_kernel(density_ref, pattern_ref, row_ref):
    block, width = density_ref.shape
    slots = pattern_ref.shape[1]
    flags = jnp.concatenate(
        [pattern_ref[...].astype(jnp.float32), jnp.zeros((1, block - slots), jnp.float32)], axis=1
    )
    flags = jnp.broadcast_to(flags, (block, block)).astype(jnp.bfloat16)
    parity = (lax.axis_index("row") * lax.axis_size("col") + lax.axis_index("col")) % 2
    low = density_ref[...].astype(jnp.bfloat16)

    @pl.when(parity == 0)
    def _():
        row_ref[:, :block] = flags
        row_ref[:, block:] = low

    @pl.when(parity == 1)
    def _():
        row_ref[:, :width] = low
        row_ref[:, width:] = flags


def dot(left, right, on=0):
    return lax.dot_general(left, right, (((1,), (on,)), ((), ())), preferred_element_type=jnp.float32)


def purify_kernel(block, half, copies, *refs):
    count = len(refs) - 7
    pieces, out_ref = refs[:count], refs[count]
    band_ref, next_ref, flag_ref, mask_ref, square_ref, low_ref = refs[count + 1 :]
    slots = 2 * half + 1
    width = (slots + 1) * block
    reach = 4 * half + 2
    window = (2 * half + 4) * block
    panel = 4 * block
    bits = jnp.bfloat16
    place = lax.axis_index("row") * lax.axis_size("col") + lax.axis_index("col")
    local, start = place % GROUP, place // GROUP * GROUP
    parity = local % 2
    origin = place - parity - 2 * half

    left = 10 * block
    flag_ref[...] = jnp.zeros_like(flag_ref)

    def clear(ref, row, first, last, column):
        if first < last:
            shape = (block, (last - first) * block)
            ref[row * block : (row + 1) * block, column + first * block : column + last * block] = jnp.zeros(shape, bits)

    for row in range(reach):
        first, tile = (row + 1) // 2 * 2 - half - 1, (row - half) // 4 * 4
        clear(band_ref, row, max(0, tile), max(0, first), left)
        clear(band_ref, row, min(reach, first + slots + 1), min(reach, tile + 2 * half + 4), left)

        @pl.when((origin + row < 0) | (origin + row >= lax.axis_size("row") * lax.axis_size("col")))
        def _():
            clear(band_ref, row, first, first + slots + 1, left)

    for row in range(half, half + 20):
        clear(next_ref, row, 0, 2, 0)
        for m in range(5):
            if not 4 * m <= row < 4 * m + 2 * half + 4:
                clear(next_ref, row, 4 * m + 2, 4 * m + 6, 0)
    lanes = lax.broadcasted_iota(jnp.int32, (block, 128), 1)

    def put(piece, index, odd):
        offset = index - origin

        @pl.when((offset >= 0) & (offset < reach))
        def _():
            rows = pl.ds(pl.multiple_of(offset * block, block), block)
            column = pl.multiple_of((offset + 1) // 2 * 128, 128)
            low = (1 - odd) * block
            head = piece[:, :128].astype(jnp.float32)
            tail = piece[:, width - 128 :].astype(jnp.float32)
            head_kept = lanes >= low
            tail_kept = lanes < low + block
            band_ref[rows, pl.ds(column, 128)] = jnp.where(head_kept, head, 0.0).astype(bits)
            band_ref[rows, pl.ds(column + 128, width - 256)] = piece[:, 128 : width - 128]
            band_ref[rows, pl.ds(column + width - 128, 128)] = jnp.where(tail_kept, tail, 0.0).astype(bits)
            flags = jnp.where(head_kept, 0.0, head) + jnp.where(tail_kept, 0.0, tail)
            flag_ref[pl.ds(offset, 1), :] = flags[:1]

    each = count // copies
    for copy in range(copies):
        shift = start + (0, -GROUP, GROUP)[copy]
        held = [
            piece.at[pl.ds(at, block), :]
            for piece in pieces[each * copy : each * copy + each]
            for at in range(0, piece.shape[0], block)
        ]
        for core in range(2):
            odd = parity if core == 0 else 1 - parity
            flip = first_flip(odd)
            for number, (step, one, two) in enumerate(HELD):
                base = (local & ~13) | ((((local >> 2) & 3) + 4 - step) % 4 << 2) | odd
                put(held[16 * core + number], shift + (base ^ (one * flip + two * (18 - flip))), odd)

    shape = (128, mask_ref.shape[1])
    lane = lax.broadcasted_iota(jnp.int32, shape, 0)
    slot = lane % block
    spread = (lax.broadcasted_iota(jnp.int32, shape, 1) // block == slot + lane // block + 4) & (slot < slots)
    mask_ref[...] = dot(flag_ref[...].astype(bits), spread.astype(bits))

    spans = [(0, 1, 0, 10), (1, 4, 0, 14), (5, 4, 0, 18), (9, 4, 0, 22), (13, 4, 4, 22), (17, 4, 8, 22), (21, 1, 12, 22)]

    for m in range(5):

        def kept(first, size):
            rows = []
            for w in range(first, first + size):
                column = (22 + w % 2 - w) * block
                row = mask_ref[4 * m + w : 4 * m + w + 1, column : column + panel]
                rows.append(jnp.broadcast_to(row, (block, panel)))
            return jnp.concatenate(rows, axis=0)

        def rows(first, size, low, high):
            at = 4 * m * block
            columns = slice(left + at + low * block, left + at + high * block)
            return band_ref[at + first * block : at + (first + size) * block, columns]

        for step, (first, size, low, high) in enumerate(spans):
            span = slice(first * block, (first + size) * block)
            other = m + step - 3
            if size == 4 and 0 <= other < m:
                mirrored = (9 + 4 * (m - other)) * block
                square = square_ref[other, mirrored : mirrored + panel, :].T
            else:
                square = kept(first, size) * dot(rows(first, size, low, high), rows(half, 4, low, high), 1)
            square_ref[m, span, :] = square
            low_ref[m, span, :] = square.astype(bits)
        for first, size, low, high in spans:
            if half <= 4 * m + first < half + 20:
                span = slice(first * block, (first + size) * block)
                cube = dot(rows(first, size, low, high), low_ref[m, low * block : high * block, :])
                current = kept(first, size) * (3.0 * square_ref[m, span, :] - 2.0 * cube)
                at = 4 * m * block
                next_ref[at + span.start : at + span.stop, at + 2 * block : at + 6 * block] = current.astype(bits)

    inner = slice(half * block, (half + 20) * block)
    chosen = lax.broadcasted_iota(jnp.int32, (block, panel), 1)
    chosen = chosen == lax.broadcasted_iota(jnp.int32, (block, panel), 0) + (1 + parity) * block
    mine = dot(chosen.astype(bits), next_ref[inner, 10 * block : 14 * block], 1).astype(bits)
    kept = mask_ref[pl.ds(2 * half + parity, 1), 2 * block : 2 * block + window]

    def times_next(value):
        parts = []
        for n in range(0, window, panel):
            low = max(0, n // block - half - 2) // 2 * 2 * block
            high = min(20, -(-(n // block + half + 2) // 2) * 2) * block
            rows = slice(half * block + low, half * block + high)
            parts.append(dot(value[:, low:high], next_ref[rows, n : min(n + panel, window)]))
        return jnp.concatenate(parts, axis=1)

    square = kept * times_next(mine)
    cube = times_next(square.astype(bits)[:, 2 * block :])
    current = kept * (3.0 * square - 2.0 * cube)
    out_ref[...] = jnp.where(
        parity == 0,
        current[:, 2 * block : (slots + 2) * block],
        current[:, 3 * block : (slots + 3) * block],
    )


def local(density, pattern):
    block, width = density.shape
    slots = pattern.shape[1]
    half = (slots - 1) // 2
    count = lax.axis_size("row") * lax.axis_size("col")
    row = pl.pallas_call(
        prepare_kernel,
        out_shape=pltpu.VMEM((block, width + block), jnp.bfloat16),
        in_specs=[pl.BlockSpec(memory_space=pltpu.VMEM)] * 2,
        out_specs=pl.BlockSpec(memory_space=pltpu.VMEM),
    )(density, pattern)
    pieces = gather(row, count)
    copies = 1
    if count > GROUP:
        pieces = (
            pieces
            + [send(piece, count, lambda d: d + GROUP) for piece in pieces]
            + [send(piece, count, lambda d: d - GROUP) for piece in pieces]
        )
        copies = 3

    def kernel(*refs):
        purify_kernel(block, half, copies, *refs)

    window = (2 * half + 4) * block
    reach = (4 * half + 2) * block
    return pl.pallas_call(
        kernel,
        out_shape=jax.ShapeDtypeStruct((block, width), jnp.float32),
        in_specs=[pl.BlockSpec(memory_space=pltpu.VMEM)] * len(pieces),
        out_specs=pl.BlockSpec(memory_space=pltpu.VMEM),
        scratch_shapes=[
            pltpu.VMEM((reach, (6 * half + 4) * block), jnp.bfloat16),
            pltpu.VMEM((reach, window), jnp.bfloat16),
            pltpu.VMEM((40, 128), jnp.float32),
            pltpu.VMEM((40, 26 * block), jnp.float32),
            pltpu.VMEM((5, window, 4 * block), jnp.float32),
            pltpu.VMEM((5, window, 4 * block), jnp.bfloat16),
        ],
        compiler_params=pltpu.CompilerParams(vmem_limit_bytes=44 * 2**20),
    )(*pieces)


def solution(mesh):
    placed = (P(AXES, None), P(AXES, None))
    return jax.shard_map(local, mesh=mesh, in_specs=placed, out_specs=P(AXES, None), check_vma=False)
```

```python
import jax
import jax.numpy as jnp
from jax import lax
from jax.experimental import pallas as pl
from jax.experimental.pallas import tpu as pltpu
from jax.sharding import PartitionSpec as P

AXES = ("row", "col")
GROUP = 32
HELD = ((0, 1, 0), (0, 0, 1), (0, 1, 1), (2, 0, 0), (1, 0, 0), (3, 0, 0), (1, 1, 0), (3, 1, 0))
HELD += ((1, 0, 1), (3, 0, 1), (1, 1, 1), (3, 1, 1), (2, 1, 0), (2, 0, 1), (2, 1, 1), (0, 0, 0))


def after(value, *earlier):
    return lax.optimization_barrier((value,) + earlier)[0]


def join(*parts):
    return jnp.concatenate(parts, axis=0)


def send(value, count, target):
    pairs = [(source, target(source)) for source in range(count)]
    return lax.ppermute(value, AXES, [(s, t) for s, t in pairs if 0 <= t < count])


def along_z(value, count, step):
    return send(value, count, lambda d: (d & ~12) | (((d >> 2) + step) % 4 << 2))


def first_flip(parity):
    return 2 + 14 * parity


def flip_first(value, count):
    return send(value, count, lambda d: d ^ first_flip(d & 1))


def flip_second(value, count):
    return send(value, count, lambda d: d ^ (18 - first_flip(d & 1)))


def flip_core(value, count):
    return send(value, count, lambda d: d ^ 1)


def gather(row, count):
    first = flip_first(row, count)
    near = along_z(row, count, 1)
    next_near = along_z(row, count, 3)
    second = flip_second(join(row, first), count)
    far = along_z(after(row, first), count, 2)
    far_last = along_z(second[second.shape[0] // 2 :], count, 2)
    pair = join(near, next_near)
    pair_first = flip_first(pair, count)
    pair_second = flip_second(after(pair, second), count)
    pair_last = flip_second(pair_first, count)
    far_first = flip_first(far, count)
    far_second = flip_second(far, count)
    pieces = [first, second, far, pair, pair_first, pair_second, pair_last, far_first, far_second, far_last, row]
    return pieces + [flip_core(after(piece, far_last) if piece is pair_first else piece, count) for piece in pieces]


def prepare_kernel(density_ref, pattern_ref, row_ref):
    block, width = density_ref.shape
    slots = pattern_ref.shape[1]
    flags = jnp.concatenate(
        [pattern_ref[...].astype(jnp.float32), jnp.zeros((1, block - slots), jnp.float32)], axis=1
    )
    flags = jnp.broadcast_to(flags, (block, block)).astype(jnp.bfloat16)
    parity = (lax.axis_index("row") * lax.axis_size("col") + lax.axis_index("col")) % 2
    low = density_ref[...].astype(jnp.bfloat16)

    @pl.when(parity == 0)
    def _():
        row_ref[:, :block] = flags
        row_ref[:, block:] = low

    @pl.when(parity == 1)
    def _():
        row_ref[:, :width] = low
        row_ref[:, width:] = flags


def dot(left, right, on=0):
    return lax.dot_general(left, right, (((1,), (on,)), ((), ())), preferred_element_type=jnp.float32)


def purify_kernel(block, half, copies, *refs):
    count = len(refs) - 7
    pieces, out_ref = refs[:count], refs[count]
    band_ref, next_ref, flag_ref, mask_ref, square_ref, low_ref = refs[count + 1 :]
    slots = 2 * half + 1
    width = (slots + 1) * block
    reach = 4 * half + 2
    window = (2 * half + 4) * block
    panel = 4 * block
    bits = jnp.bfloat16
    place = lax.axis_index("row") * lax.axis_size("col") + lax.axis_index("col")
    local, start = place % GROUP, place // GROUP * GROUP
    parity = local % 2
    origin = place - parity - 2 * half

    left = 10 * block
    flag_ref[...] = jnp.zeros_like(flag_ref)

    def clear(ref, row, first, last, column):
        if first < last:
            shape = (block, (last - first) * block)
            ref[row * block : (row + 1) * block, column + first * block : column + last * block] = jnp.zeros(shape, bits)

    for row in range(reach):
        first, tile = (row + 1) // 2 * 2 - half - 1, (row - half) // 4 * 4
        clear(band_ref, row, max(0, tile), max(0, first), left)
        clear(band_ref, row, min(reach, first + slots + 1), min(reach, tile + 2 * half + 4), left)

        @pl.when((origin + row < 0) | (origin + row >= lax.axis_size("row") * lax.axis_size("col")))
        def _():
            clear(band_ref, row, first, first + slots + 1, left)

    for row in range(half, half + 20):
        clear(next_ref, row, 0, 2, 0)
        for m in range(5):
            if not 4 * m <= row < 4 * m + 2 * half + 4:
                clear(next_ref, row, 4 * m + 2, 4 * m + 6, 0)
    lanes = lax.broadcasted_iota(jnp.int32, (block, 128), 1)

    def put(piece, index, odd):
        offset = index - origin

        @pl.when((offset >= 0) & (offset < reach))
        def _():
            rows = pl.ds(pl.multiple_of(offset * block, block), block)
            column = pl.multiple_of((offset + 1) // 2 * 128, 128)
            low = (1 - odd) * block
            head = piece[:, :128].astype(jnp.float32)
            tail = piece[:, width - 128 :].astype(jnp.float32)
            head_kept = lanes >= low
            tail_kept = lanes < low + block
            band_ref[rows, pl.ds(column, 128)] = jnp.where(head_kept, head, 0.0).astype(bits)
            band_ref[rows, pl.ds(column + 128, width - 256)] = piece[:, 128 : width - 128]
            band_ref[rows, pl.ds(column + width - 128, 128)] = jnp.where(tail_kept, tail, 0.0).astype(bits)
            flags = jnp.where(head_kept, 0.0, head) + jnp.where(tail_kept, 0.0, tail)
            flag_ref[pl.ds(offset, 1), :] = flags[:1]

    each = count // copies
    for copy in range(copies):
        shift = start + (0, -GROUP, GROUP)[copy]
        held = [
            piece.at[pl.ds(at, block), :]
            for piece in pieces[each * copy : each * copy + each]
            for at in range(0, piece.shape[0], block)
        ]
        for core in range(2):
            odd = parity if core == 0 else 1 - parity
            flip = first_flip(odd)
            for number, (step, one, two) in enumerate(HELD):
                base = (local & ~13) | ((((local >> 2) & 3) + 4 - step) % 4 << 2) | odd
                put(held[16 * core + number], shift + (base ^ (one * flip + two * (18 - flip))), odd)

    shape = (128, mask_ref.shape[1])
    lane = lax.broadcasted_iota(jnp.int32, shape, 0)
    slot = lane % block
    spread = (lax.broadcasted_iota(jnp.int32, shape, 1) // block == slot + lane // block + 4) & (slot < slots)
    mask_ref[...] = dot(flag_ref[...].astype(bits), spread.astype(bits))

    spans = [(0, 1, 0, 10), (1, 4, 0, 14), (5, 4, 0, 18), (9, 4, 0, 22), (13, 4, 4, 22), (17, 4, 8, 22), (21, 1, 12, 22)]

    def step_one(m, cubes):
        def kept(first, size):
            rows = []
            for w in range(first, first + size):
                column = (22 + w % 2 - w) * block
                row = mask_ref[4 * m + w : 4 * m + w + 1, column : column + panel]
                rows.append(jnp.broadcast_to(row, (block, panel)))
            return jnp.concatenate(rows, axis=0)

        def rows(first, size, low, high):
            at = 4 * m * block
            columns = slice(left + at + low * block, left + at + high * block)
            return band_ref[at + first * block : at + (first + size) * block, columns]

        for step, (first, size, low, high) in enumerate([] if cubes else spans):
            span = slice(first * block, (first + size) * block)
            other = m + step - 3
            if size == 4 and 0 <= other < m:
                mirrored = (9 + 4 * (m - other)) * block
                square = square_ref[other, mirrored : mirrored + panel, :].T
            else:
                square = kept(first, size) * dot(rows(first, size, low, high), rows(half, 4, low, high), 1)
            square_ref[m, span, :] = square
            low_ref[m, span, :] = square.astype(bits)
        for first, size, low, high in spans if cubes else []:
            if half <= 4 * m + first < half + 20:
                span = slice(first * block, (first + size) * block)
                cube = dot(rows(first, size, low, high), low_ref[m, low * block : high * block, :])
                current = kept(first, size) * (3.0 * square_ref[m, span, :] - 2.0 * cube)
                at = 4 * m * block
                next_ref[at + span.start : at + span.stop, at + 2 * block : at + 6 * block] = current.astype(bits)

    for m in range(6):
        if m < 5:
            step_one(m, False)
        if m > 0:
            step_one(m - 1, True)

    inner = slice(half * block, (half + 20) * block)
    chosen = lax.broadcasted_iota(jnp.int32, (block, panel), 1)
    chosen = chosen == lax.broadcasted_iota(jnp.int32, (block, panel), 0) + (1 + parity) * block
    mine = dot(chosen.astype(bits), next_ref[inner, 10 * block : 14 * block], 1).astype(bits)
    kept = mask_ref[pl.ds(2 * half + parity, 1), 2 * block : 2 * block + window]

    def times_next(value):
        parts = []
        for n in range(0, window, panel):
            low = max(0, n // block - half - 2) // 2 * 2 * block
            high = min(20, -(-(n // block + half + 2) // 2) * 2) * block
            rows = slice(half * block + low, half * block + high)
            parts.append(dot(value[:, low:high], next_ref[rows, n : min(n + panel, window)]))
        return jnp.concatenate(parts, axis=1)

    square = kept * times_next(mine)
    cube = times_next(square.astype(bits)[:, 2 * block :])
    current = kept * (3.0 * square - 2.0 * cube)
    out_ref[...] = jnp.where(
        parity == 0,
        current[:, 2 * block : (slots + 2) * block],
        current[:, 3 * block : (slots + 3) * block],
    )


def local(density, pattern):
    block, width = density.shape
    slots = pattern.shape[1]
    half = (slots - 1) // 2
    count = lax.axis_size("row") * lax.axis_size("col")
    row = pl.pallas_call(
        prepare_kernel,
        out_shape=pltpu.VMEM((block, width + block), jnp.bfloat16),
        in_specs=[pl.BlockSpec(memory_space=pltpu.VMEM)] * 2,
        out_specs=pl.BlockSpec(memory_space=pltpu.VMEM),
    )(density, pattern)
    pieces = gather(row, count)
    copies = 1
    if count > GROUP:
        pieces = (
            pieces
            + [send(piece, count, lambda d: d + GROUP) for piece in pieces]
            + [send(piece, count, lambda d: d - GROUP) for piece in pieces]
        )
        copies = 3

    def kernel(*refs):
        purify_kernel(block, half, copies, *refs)

    window = (2 * half + 4) * block
    reach = (4 * half + 2) * block
    return pl.pallas_call(
        kernel,
        out_shape=jax.ShapeDtypeStruct((block, width), jnp.float32),
        in_specs=[pl.BlockSpec(memory_space=pltpu.VMEM)] * len(pieces),
        out_specs=pl.BlockSpec(memory_space=pltpu.VMEM),
        scratch_shapes=[
            pltpu.VMEM((reach, (6 * half + 4) * block), jnp.bfloat16),
            pltpu.VMEM((reach, window), jnp.bfloat16),
            pltpu.VMEM((40, 128), jnp.float32),
            pltpu.VMEM((40, 26 * block), jnp.float32),
            pltpu.VMEM((5, window, 4 * block), jnp.float32),
            pltpu.VMEM((5, window, 4 * block), jnp.bfloat16),
        ],
        compiler_params=pltpu.CompilerParams(vmem_limit_bytes=44 * 2**20),
    )(*pieces)


def solution(mesh):
    placed = (P(AXES, None), P(AXES, None))
    return jax.shard_map(local, mesh=mesh, in_specs=placed, out_specs=P(AXES, None), check_vma=False)
```
